32 devices in a mesh: lblk: 16 (over z, x, core), tile: 2 (over y).
Axes of the slice: x: 2, y: 2, z: 4, core: 2. Of those that a mesh axis runs over, the one named last changes fastest.
Arguments:
- wavefunction: float32 [2048, 2, 16, 128], P('lblk', None, 'tile'), may hold values from -6 to 6
- l_table: int32 [2048, 2], P('lblk'), may hold values from 0 to 15
- coupling: float32 [16, 8, 128, 128], P('lblk'), may hold values from -2 to 2
- selection: int32 [16, 8], P('lblk'), may hold values 0 or 1
- dipole: float32 [16, 2, 128, 128], P('lblk'), may hold values from -0.5 to 0.5
- field: float32 [1], replicated, may hold values from -0.1 to 0.1
Outputs:
- propagated: float32 [2048, 2, 16, 128], P('lblk', None, 'tile')
The draws below stay inside these ranges and needn't reach their ends.
All inputs are finite; a program needn't handle non-finite values. No bound on the sum of `selection` on one device may be relied on, other than what follows from the above.
Results may differ from the reference program's by a relative error of at most 0.0001.
Values sent between devices are 32-bit elements; how exact they have to be, the bound alone decides.
A program may use at most 64 MiB of HBM per device.

```python
import jax
import jax.numpy as jnp
from jax import lax

CH = 128
NMP = 8
R2 = 128
TAYLOR = 4
STEPS = 1
NL = 16
NR1 = 16


def draw_wavefunction(key, part):
    key_sign, key_amp = jax.random.split(jax.random.fold_in(key, 11))
    rows = jnp.arange(NR1)
    cols = jnp.arange(R2)
    parity = (1 - 2 * ((rows[:, None] + cols[None, :]) % 2)).astype(jnp.float32)
    part_sign = jnp.where(jax.random.bernoulli(key_sign, 0.5, (1, 2, 1, 1)), 1.0, -1.0).astype(jnp.float32)
    shape = (NL * CH, 2, NR1, R2)
    amplitude = jax.random.uniform(key_amp, shape, jnp.float32, 0.5, 2.5)
    return amplitude * part_sign * parity[None, None]


def draw_coupling(key, part):
    key_sign, key_val = jax.random.split(jax.random.fold_in(key, 23))
    row_sign = jnp.where(jax.random.bernoulli(key_sign, 0.5, (NL, NMP, CH, 1)), 1.0, -1.0).astype(jnp.float32)
    shape = (NL, NMP, CH, CH)
    values = 0.12 + 0.25 * jax.random.normal(key_val, shape, jnp.float32)
    return jnp.clip(row_sign * values, -2.0, 2.0)


def set_ends(values, own_key, least, top_value):
    dims = values.shape
    index_at = [jax.random.randint(jax.random.fold_in(own_key, axis), (), 0, dims[axis]) for axis in range(len(dims))]
    values = values.at[tuple(index_at)].set(least)
    longest = dims.index(max(dims))
    index_at[longest] = (index_at[longest] + 1) % dims[longest]
    return values.at[tuple(index_at)].set(top_value)


def block_scale(rng, shape, cuts, smallest, largest):
    def one(axis_at, blocks):
        heights = jax.random.uniform(jax.random.fold_in(jax.random.fold_in(rng, 6), axis_at), (blocks,), jnp.float32, smallest / len(cuts), largest / len(cuts))
        return jnp.repeat(jnp.exp(heights), shape[axis_at] // blocks).reshape((-1,) + (1,) * (len(shape) - axis_at - 1))

    loudness = one(*cuts[0])
    for cut in cuts[1:]:
        loudness = loudness * one(*cut)
    return loudness


def centred(rng, shape, width, bound, shards=(), dtype=jnp.bfloat16):
    array = width * jax.random.normal(rng, shape, jnp.float32)
    if shards:
        array = array * block_scale(rng, shape, shards, -0.22, 0.18)
    return jnp.clip(array, -bound, bound).astype(dtype)


def setup_inputs(seed: int = 0) -> dict:
    keys = jax.random.split(jax.random.key(seed), 7)
    return {
        "wavefunction": draw_wavefunction(jax.random.fold_in(keys[6], 71), 0),
        "l_table": set_ends(jax.random.randint(keys[1], (NL * CH, 2), 0, 16), jax.random.fold_in(keys[1], 1), 0, 15).astype(jnp.int32),
        "coupling": draw_coupling(jax.random.fold_in(keys[6], 71), 0),
        "selection": set_ends((jax.random.randint(keys[3], (NL, NMP), 0, 4) < 3).astype(jnp.int32), jax.random.fold_in(keys[3], 1), 0, 1),
        "dipole": centred(keys[4], (NL, 2, CH, CH), CH ** -0.5, 0.5, ((0, 16),), jnp.float32),
        "field": jnp.clip(jax.random.uniform(keys[5], (STEPS,), jnp.float32, -0.1, 0.1), -0.1, 0.1),
    }


time_step = 0.03
grid_step = 0.5
radius_start = 8.0


def second_diff(padded, along, length_along):
    def window(offset):
        return lax.slice_in_dim(padded, offset, offset + length_along, axis=along)
    return (-window(0) + 16.0 * window(1) - 30.0 * window(2) + 16.0 * window(3) - window(4)) / (12.0 * grid_step * grid_step)


def mat_product(matrix, field_in):
    flat = field_in.reshape(field_in.shape[0], -1)
    out = jnp.dot(matrix, flat, precision=lax.Precision.HIGHEST, preferred_element_type=jnp.float32)
    return out.reshape(field_in.shape)


def reference(wavefunction, l_table, coupling, selection, dipole, field):
    row_count = wavefunction.shape[2]
    col_count = wavefunction.shape[3]
    channels = CH
    radius_one = radius_start + grid_step * jnp.arange(row_count).astype(jnp.float32)
    radius_two = radius_start + grid_step * jnp.arange(col_count).astype(jnp.float32)
    larger = jnp.maximum(radius_one[:, None], radius_two[None, :])
    smaller = jnp.minimum(radius_one[:, None], radius_two[None, :])
    orders = jnp.arange(NMP).astype(jnp.float32)
    radial = (smaller / larger)[None] ** orders[:, None, None] / larger[None]
    weights = 0.5 * (coupling + jnp.swapaxes(coupling, 2, 3)) * selection.astype(jnp.float32)[:, :, None, None]
    angular = l_table.astype(jnp.float32).reshape(NL, channels, 2)
    base_pot = -2.0 / radius_one[:, None] - 2.0 / radius_two[None, :]
    dip_low = jnp.pad(dipole, ((1, 0), (0, 0), (0, 0), (0, 0)))[:-1]
    scale_one = radius_one[None, None, :, None]
    scale_two = radius_two[None, None, None, :]

    def hamiltonian(series_term, strength):
        blocks = series_term.reshape(NL, channels, 2, row_count, col_count)
        padded_l = jnp.pad(blocks, ((1, 1), (0, 0), (0, 0), (0, 0), (0, 0)))
        block_above = padded_l[2:]
        block_below = padded_l[:-2]

        def one_block(items):
            field_in, upper_in, lower_in, weight_blk, coupling_up, coupling_down, ang = items
            pad_one = jnp.pad(field_in, ((0, 0), (0, 0), (2, 2), (0, 0)))
            pad_two = jnp.pad(field_in, ((0, 0), (0, 0), (0, 0), (2, 2)))
            laplace_sum = second_diff(pad_one, 2, row_count) + second_diff(pad_two, 3, col_count)
            cent = (ang[:, 0] * (ang[:, 0] + 1.0) / 2.0)[:, None, None] / (radius_one[None, :, None] ** 2) + (ang[:, 1] * (ang[:, 1] + 1.0) / 2.0)[:, None, None] / (radius_two[None, None, :] ** 2)
            potential = base_pot[None] + cent
            result = -0.5 * laplace_sum + potential[:, None] * field_in
            for multi in range(NMP):
                result = result + mat_product(weight_blk[multi], radial[multi][None, None] * field_in)
            dipole_term = mat_product(coupling_up[0], scale_one * upper_in) + mat_product(coupling_up[1], scale_two * upper_in)
            dipole_term = dipole_term + mat_product(coupling_down[0].T, scale_one * lower_in) + mat_product(coupling_down[1].T, scale_two * lower_in)
            return result + strength * dipole_term

        applied = lax.map(one_block, (blocks, block_above, block_below, weights, dipole, dip_low, angular))
        return applied.reshape(series_term.shape)

    total = wavefunction
    for step_index in range(STEPS):
        strength = field[step_index]
        series_term = total
        accum = total
        for order_index in range(1, TAYLOR + 1):
            applied = hamiltonian(series_term, strength)
            series_term = (time_step / order_index) * jnp.stack([applied[:, 1], -applied[:, 0]], axis=1)
            accum = accum + series_term
        total = accum
    return total
```

```python
import functools

import jax
import jax.numpy as jnp
from jax import lax
from jax.experimental import pallas as pl
from jax.experimental.pallas import tpu as pltpu
from jax.sharding import PartitionSpec as P

TAYLOR = 4
time_step = 0.03
grid_step = 0.5
radius_start = 8.0
F32 = jnp.float32
BF16 = jnp.bfloat16
MESH = pl.DeviceIdType.MESH
HALO = 2
ROWS = 2


def halves(value):
    high = value.astype(BF16)
    return high, (value - high.astype(F32)).astype(BF16)


def three_pass(value_list):
    pairs = [halves(value) for value in value_list]
    high = [pair[0] for pair in pairs]
    return jnp.concatenate(high + high + [pair[1] for pair in pairs], axis=0)


def kernel(
    blocks, tiles, cols, wave, angular, coupling, dipole, selection, field, out,
    state, near, weights, lower, w_stack, d_stack, part, totals, from_pair,
    psi_sem, wgt_sem, core_sem, z_sem, down_sem, up_sem, dcore_sem, dz_sem, back_sem,
):
    ch = coupling.shape[1]
    nmp = coupling.shape[0]
    quad = nmp // 2
    width = wave.shape[2]
    rows = width // cols
    edge = HALO * cols
    mid = pl.ds(edge, width)

    me = lax.axis_index("lblk")
    tile = lax.axis_index("tile")
    core = me % 2
    pair = (me // 2) % 2
    other = 1 - pair
    quad_at = me // 4
    last_quad = blocks // 4 - 1
    to_pair = {"lblk": me + 2 - 4 * pair}
    to_core = {"lblk": me + 1 - 2 * core}
    to_z = {"lblk": me + 6 * core - 3}
    to_low = {"tile": tile - 1}
    to_high = {"tile": tile + 1}
    has_z = jnp.logical_or(
        jnp.logical_and(core == 1, quad_at < last_quad), jnp.logical_and(core == 0, quad_at > 0)
    )
    has_low = tile > 0
    has_high = tile < tiles - 1

    def remote(src, dst, sems, target):
        return pltpu.make_async_remote_copy(
            src_ref=src, dst_ref=dst, send_sem=sems.at[0], recv_sem=sems.at[1],
            device_id=target, device_id_type=MESH,
        )

    def psi_copy():
        return remote(wave.at[other], state.at[0, pair, :, mid], psi_sem, to_pair)

    def weight_copy():
        return remote(weights.at[pair], weights.at[pair], wgt_sem, to_pair)

    def core_copy(step, b):
        return remote(state.at[step, b, :, mid], near.at[step, core + b], core_sem.at[step, b], to_core)

    def z_copy(step):
        return remote(state.at[step, core, :, mid], near.at[step, 2 * (1 - core)], z_sem.at[step], to_z)

    def low_copy(step, b):
        return remote(
            state.at[step, b, :, pl.ds(edge, edge)], state.at[step, b, :, pl.ds(edge + width, edge)],
            down_sem.at[step, b], to_low,
        )

    def high_copy(step, b):
        return remote(
            state.at[step, b, :, pl.ds(width, edge)], state.at[step, b, :, pl.ds(0, edge)],
            up_sem.at[step, b], to_high,
        )

    def send_block(step, b):
        @pl.when(jnp.logical_and(b == core, has_z))
        def _():
            z_copy(step).start()

        @pl.when(has_low)
        def _():
            low_copy(step, b).start()

        @pl.when(has_high)
        def _():
            high_copy(step, b).start()

        core_copy(step, b).start()

    def wait_sent(step, b):
        @pl.when(jnp.logical_and(b == core, has_z))
        def _():
            z_copy(step).wait_send()

        @pl.when(has_low)
        def _():
            low_copy(step, b).wait_send()

        @pl.when(has_high)
        def _():
            high_copy(step, b).wait_send()

        core_copy(step, b).wait_send()

    def wait_halo(step, b):
        @pl.when(has_high)
        def _():
            low_copy(step, b).wait_recv()

        @pl.when(has_low)
        def _():
            high_copy(step, b).wait_recv()

    def back_copy(which):
        return remote(totals.at[which, other], from_pair.at[which], back_sem.at[which], to_pair)

    def dcore_low(b):
        return remote(weights.at[b, pl.ds(nmp, 2)], lower.at[b], dcore_sem.at[b], to_core)

    def dcore_high():
        return remote(weights.at[0, pl.ds(nmp, 2)], lower.at[1], dcore_sem.at[1], to_core)

    def dz_copy():
        return remote(weights.at[1, pl.ds(nmp, 2)], lower.at[0], dz_sem, to_z)

    barrier = pltpu.get_barrier_semaphore()
    for target, there in (
        (to_pair, None), (to_core, None), (to_z, has_z), (to_low, has_low), (to_high, has_high),
    ):
        if there is None:
            pl.semaphore_signal(barrier, inc=1, device_id=target, device_id_type=MESH)
        else:
            @pl.when(there)
            def _(target=target):
                pl.semaphore_signal(barrier, inc=1, device_id=target, device_id_type=MESH)
    state[0, pair, :, mid] = wave[pair]
    peers = 2
    for there in (has_z, has_low, has_high):
        peers = peers + there.astype(jnp.int32)
    pl.semaphore_wait(barrier, peers)

    psi_copy().start()
    send_block(0, pair)

    for k in range(nmp):
        weights[pair, k] = (0.5 * selection[0, k].astype(F32)) * (coupling[k] + coupling[k].T)
    weights[pair, nmp] = dipole[0]
    weights[pair, nmp + 1] = dipole[1]
    lane = lax.broadcasted_iota(jnp.int32, (ch, ch), 1)
    momenta = angular[...].astype(F32)
    momenta = 0.5 * momenta * (momenta + 1.0)
    weights[pair, nmp + 2] = jnp.where(lane < ch // 2, momenta[:, 0:1], momenta[:, 1:2])
    weight_copy().start()

    for step in range(TAYLOR):
        for b in range(2):
            @pl.when(jnp.logical_not(has_low))
            def _(step=step, b=b):
                state[step, b, :, pl.ds(0, edge)] = jnp.zeros((ch, edge), F32)

            @pl.when(jnp.logical_not(has_high))
            def _(step=step, b=b):
                state[step, b, :, pl.ds(edge + width, edge)] = jnp.zeros((ch, edge), F32)

        @pl.when(jnp.logical_not(has_z))
        def _(step=step):
            near[step, 2 * core] = jnp.zeros((ch, width), F32)

    @pl.when(jnp.logical_and(core == 0, jnp.logical_not(has_z)))
    def _():
        lower[0] = jnp.zeros((2, ch, ch), F32)

    def stack_weights(b):
        for a in range(quad):
            at = pl.ds(a * ch, ch)
            for part_at, k in ((0, a), (1, a + quad)):
                high, low = halves(weights[b, k])
                w_stack[b, at, pl.ds(part_at * ch, ch)] = high
                w_stack[b, at, pl.ds((2 + part_at) * ch, ch)] = low
                w_stack[b, at, pl.ds((4 + part_at) * ch, ch)] = high

    def stack_dipoles(b):
        for a in range(2):
            at = pl.ds(a * ch, ch)
            for part_at, matrix in ((0, weights[b, nmp + a]), (1, lower[b, a].T)):
                high, low = halves(matrix)
                d_stack[b, at, pl.ds(part_at * ch, ch)] = high
                d_stack[b, at, pl.ds((2 + part_at) * ch, ch)] = low
                d_stack[b, at, pl.ds((4 + part_at) * ch, ch)] = high

    span = ROWS * cols

    def radii(at):
        index = lax.broadcasted_iota(jnp.int32, (1, span), 1)
        row = tile * rows + at * ROWS + index // cols
        one = radius_start + grid_step * row.astype(F32)
        two = radius_start + grid_step * (index % cols).astype(F32)
        return one, two

    def multipoles(step, b):
        def body(at, carry):
            one, two = radii(at)
            larger = jnp.maximum(one, two)
            ratio = jnp.minimum(one, two) / larger
            power = ratio
            for _ in range(quad - 1):
                power = power * ratio
            value = state[step, b, :, pl.ds(pl.multiple_of(edge + at * span, cols), span)]
            stacked = three_pass([value, power * value])
            product = jnp.dot(w_stack[b], stacked, preferred_element_type=F32)
            result = product[(quad - 1) * ch:]
            for a in range(quad - 2, -1, -1):
                result = product[a * ch:(a + 1) * ch] + ratio * result
            part[b, :, pl.ds(pl.multiple_of(at * span, cols), span)] = result / larger
            return carry

        lax.fori_loop(0, rows // ROWS, body, 0)

    def finish(step, b, scale):
        strength = field[0]
        c_one = weights[b, nmp + 2, :, 0:1]
        c_two = weights[b, nmp + 2, :, ch // 2:ch // 2 + 1]
        lane_at = lax.broadcasted_iota(jnp.int32, (1, cols), 1)

        def body(at, carry):
            one, two = radii(at)
            here = pl.ds(pl.multiple_of(at * span, cols), span)
            up = near[step, b + 1, :, here]
            down = near[step, b, :, here]
            product = jnp.dot(d_stack[b], three_pass([up, down]), preferred_element_type=F32)
            dipole_term = (strength * one) * product[:ch] + (strength * two) * product[ch:]

            def window(offset):
                start = pl.multiple_of(at * span + (HALO + offset) * cols, cols)
                return state[step, b, :, pl.ds(start, span)]

            value = window(0)
            around = 16.0 * (window(-1) + window(1)) - (window(-2) + window(2))
            pieces = []
            for r in range(ROWS):
                line = value[:, r * cols:(r + 1) * cols]

                def moved(by):
                    rolled = pltpu.roll(line, by % cols, 1)
                    inside = lane_at >= by if by > 0 else lane_at < cols + by
                    return jnp.where(inside, rolled, 0.0)

                pieces.append(16.0 * (moved(1) + moved(-1)) - (moved(2) + moved(-2)))
            around = around + jnp.concatenate(pieces, axis=1)
            factor = -0.5 / (12.0 * grid_step * grid_step)
            centre = (
                (-60.0 * factor) - 2.0 / one - 2.0 / two + c_one / (one * one) + c_two / (two * two)
            )
            applied = factor * around + centre * value + part[b, :, here] + dipole_term
            term = scale * applied
            start = pl.multiple_of(edge + at * span, cols)
            state[step + 1, b, :, pl.ds(start, span)] = term
            which = (step + 1) % 2
            totals[which, b, :, here] = totals[which, b, :, here] + term
            return carry

        lax.fori_loop(0, rows // ROWS, body, 0)

    stack_weights(pair)
    multipoles(0, pair)
    psi_copy().wait_recv()
    send_block(0, other)
    for b in range(2):
        totals[0, b] = state[0, b, :, mid]
        totals[1, b] = jnp.zeros((ch, width), F32)
    weight_copy().wait_recv()

    @pl.when(core == 0)
    def _():
        dcore_low(0).start()
        dcore_low(1).start()

    @pl.when(core == 1)
    def _():
        dcore_high().start()

        @pl.when(has_z)
        def _():
            dz_copy().start()

    stack_weights(other)
    multipoles(0, other)

    @pl.when(core == 1)
    def _():
        dcore_low(0).wait_recv()
        dcore_low(1).wait_recv()

    @pl.when(core == 0)
    def _():
        dcore_high().wait_recv()

        @pl.when(has_z)
        def _():
            dz_copy().wait_recv()

    stack_dipoles(0)
    stack_dipoles(1)

    def order(step, carry):
        @pl.when(step > 0)
        def _():
            multipoles(step, other)
            multipoles(step, pair)

        sign = ((2 * ((step + 1) % 2) - 1) * (2 * pair - 1)).astype(F32)
        scale = sign * (time_step / (step + 1).astype(F32))
        core_copy(step, 0).wait_recv()
        core_copy(step, 1).wait_recv()

        @pl.when(has_z)
        def _():
            z_copy(step).wait_recv()

        for b in (other, pair):
            wait_halo(step, b)
            finish(step, b, scale)

            @pl.when(step < TAYLOR - 1)
            def _():
                send_block(step + 1, b)

            if b is other:
                @pl.when(step >= TAYLOR - 2)
                def _():
                    back_copy((step + 1) % 2).start()
        return carry

    lax.fori_loop(0, TAYLOR, order, 0)

    back_copy(1).wait_recv()
    back_copy(0).wait_recv()
    out[pair] = totals[0, pair] + from_pair[1]
    out[other] = totals[1, pair] + from_pair[0]

    psi_copy().wait_send()
    weight_copy().wait_send()
    for step in range(TAYLOR):
        for b in range(2):
            wait_sent(step, b)

    @pl.when(core == 0)
    def _():
        dcore_low(0).wait_send()
        dcore_low(1).wait_send()

    @pl.when(core == 1)
    def _():
        dcore_high().wait_send()

        @pl.when(has_z)
        def _():
            dz_copy().wait_send()

    back_copy(0).wait_send()
    back_copy(1).wait_send()


def per_device(blocks, tiles, wavefunction, l_table, coupling, selection, dipole, field):
    ch, parts, rows, cols = wavefunction.shape
    width = rows * cols
    nmp = coupling.shape[1]
    edge = HALO * cols
    wave = jnp.transpose(wavefunction, (1, 0, 2, 3)).reshape(parts, ch, width)
    vmem = pl.BlockSpec(memory_space=pltpu.VMEM)
    smem = pl.BlockSpec(memory_space=pltpu.SMEM)
    dma = pltpu.SemaphoreType.DMA
    result = pl.pallas_call(
        functools.partial(kernel, blocks, tiles, cols),
        out_shape=jax.ShapeDtypeStruct((parts, ch, width), F32),
        in_specs=[vmem, vmem, vmem, vmem, smem, smem],
        out_specs=vmem,
        scratch_shapes=[
            pltpu.VMEM((TAYLOR + 1, 2, ch, width + 2 * edge), F32),
            pltpu.VMEM((TAYLOR, 3, ch, width), F32),
            pltpu.VMEM((2, nmp + 3, ch, ch), F32),
            pltpu.VMEM((2, 2, ch, ch), F32),
            pltpu.VMEM((2, nmp // 2 * ch, 6 * ch), BF16),
            pltpu.VMEM((2, 2 * ch, 6 * ch), BF16),
            pltpu.VMEM((2, ch, width), F32),
            pltpu.VMEM((2, 2, ch, width), F32),
            pltpu.VMEM((2, ch, width), F32),
            dma((2,)),
            dma((2,)),
            dma((TAYLOR, 2, 2)),
            dma((TAYLOR, 2)),
            dma((TAYLOR, 2, 2)),
            dma((TAYLOR, 2, 2)),
            dma((2, 2)),
            dma((2,)),
            dma((2, 2)),
        ],
        compiler_params=pltpu.CompilerParams(
            collective_id=0, has_side_effects=True, vmem_limit_bytes=48 * 1024 * 1024
        ),
    )(wave, l_table, coupling[0], dipole[0], selection, field)
    return jnp.transpose(result.reshape(parts, ch, rows, cols), (1, 0, 2, 3))


def solution(mesh):
    placed = (
        P("lblk", None, "tile", None),
        P("lblk", None),
        P("lblk", None, None, None),
        P("lblk", None),
        P("lblk", None, None, None),
        P(),
    )
    return jax.shard_map(
        functools.partial(per_device, mesh.shape["lblk"], mesh.shape["tile"]),
        mesh=mesh,
        in_specs=placed,
        out_specs=P("lblk", None, "tile", None),
        check_vma=False,
    )
```

```python
import functools

import jax
import jax.numpy as jnp
from jax import lax
from jax.experimental import pallas as pl
from jax.experimental.pallas import tpu as pltpu
from jax.sharding import PartitionSpec as P

TAYLOR = 4
time_step = 0.03
grid_step = 0.5
radius_start = 8.0
F32 = jnp.float32
BF16 = jnp.bfloat16
MESH = pl.DeviceIdType.MESH
HALO = 2
ROWS = 2


def halves(value):
    high = value.astype(BF16)
    return high, (value - high.astype(F32)).astype(BF16)


def three_pass(value_list):
    pairs = [halves(value) for value in value_list]
    high = [pair[0] for pair in pairs]
    return jnp.concatenate(high + high + [pair[1] for pair in pairs], axis=0)


def kernel(
    blocks, tiles, rows, wave_in, angular, coupling_in, dipole_in, selection, field, out,
    wave, coupling, dipole, start_other,
    state, near, weights, central, lower, w_stack, d_stack, part, totals, from_pair,
    load_sem, psi_sem, wgt_sem, core_sem, z_sem, down_sem, up_sem, dcore_sem, dz_sem, back_sem,
):
    ch = coupling.shape[1]
    nmp = coupling.shape[0]
    quad = nmp // 2
    cols = wave.shape[1]
    width = rows * cols
    stride = 2 * rows
    side = (quad + 2) * ch
    edge = HALO * cols
    mid = pl.ds(edge, width)

    me = lax.axis_index("lblk")
    tile = lax.axis_index("tile")
    core = me % 2
    pair = (me // 2) % 2
    other = 1 - pair
    quad_at = me // 4
    last_quad = blocks // 4 - 1
    to_pair = {"lblk": me + 2 - 4 * pair}
    to_core = {"lblk": me + 1 - 2 * core}
    to_z = {"lblk": me + 6 * core - 3}
    to_low = {"tile": tile - 1}
    to_high = {"tile": tile + 1}
    has_z = jnp.logical_or(
        jnp.logical_and(core == 1, quad_at < last_quad), jnp.logical_and(core == 0, quad_at > 0)
    )
    has_low = tile > 0
    has_high = tile < tiles - 1

    def remote(src, dst, sems, target):
        return pltpu.make_async_remote_copy(
            src_ref=src, dst_ref=dst, send_sem=sems.at[0], recv_sem=sems.at[1],
            device_id=target, device_id_type=MESH,
        )

    def psi_copy():
        return remote(start_other, state.at[0, pair, :, mid], psi_sem, to_pair)

    def weight_copy():
        return remote(weights.at[pair], weights.at[pair], wgt_sem, to_pair)

    def core_copy(step, b):
        return remote(state.at[step, b, :, mid], near.at[step, core + b], core_sem.at[step, b], to_core)

    def z_copy(step):
        return remote(state.at[step, core, :, mid], near.at[step, 2 * (1 - core)], z_sem.at[step], to_z)

    def low_copy(step, b):
        return remote(
            state.at[step, b, :, pl.ds(edge, edge)], state.at[step, b, :, pl.ds(edge + width, edge)],
            down_sem.at[step, b], to_low,
        )

    def high_copy(step, b):
        return remote(
            state.at[step, b, :, pl.ds(width, edge)], state.at[step, b, :, pl.ds(0, edge)],
            up_sem.at[step, b], to_high,
        )

    def send_block(step, b):
        @pl.when(jnp.logical_and(b == core, has_z))
        def _():
            z_copy(step).start()

        @pl.when(has_low)
        def _():
            low_copy(step, b).start()

        @pl.when(has_high)
        def _():
            high_copy(step, b).start()

        core_copy(step, b).start()

    def wait_sent(step, b):
        @pl.when(jnp.logical_and(b == core, has_z))
        def _():
            z_copy(step).wait_send()

        @pl.when(has_low)
        def _():
            low_copy(step, b).wait_send()

        @pl.when(has_high)
        def _():
            high_copy(step, b).wait_send()

        core_copy(step, b).wait_send()

    def wait_halo(step, b):
        @pl.when(has_high)
        def _():
            low_copy(step, b).wait_recv()

        @pl.when(has_low)
        def _():
            high_copy(step, b).wait_recv()

    def back_copy(which):
        return remote(totals.at[which, other], from_pair.at[which], back_sem.at[which], to_pair)

    def dcore_low(b):
        return remote(weights.at[b, pl.ds(quad * ch, 2 * ch)], lower.at[b], dcore_sem.at[b], to_core)

    def dcore_high():
        return remote(weights.at[0, pl.ds(quad * ch, 2 * ch)], lower.at[1], dcore_sem.at[1], to_core)

    def dz_copy():
        return remote(weights.at[1, pl.ds(quad * ch, 2 * ch)], lower.at[0], dz_sem, to_z)

    loads = [
        pltpu.make_async_copy(src, dst, load_sem.at[at])
        for at, (src, dst) in enumerate(((wave_in, wave), (coupling_in, coupling), (dipole_in, dipole)))
    ]
    for load in loads:
        load.start()

    barrier = pltpu.get_barrier_semaphore()
    for target, there in (
        (to_pair, None), (to_core, None), (to_z, has_z), (to_low, has_low), (to_high, has_high),
    ):
        if there is None:
            pl.semaphore_signal(barrier, inc=1, device_id=target, device_id_type=MESH)
        else:
            @pl.when(there)
            def _(target=target):
                pl.semaphore_signal(barrier, inc=1, device_id=target, device_id_type=MESH)
    loads[0].wait()
    for row in range(rows):
        here = pl.ds(row * cols, cols)
        start_other[:, here] = wave[pl.ds(other * rows + row, ch, stride=stride), :]
        state[0, pair, :, pl.ds(edge + row * cols, cols)] = wave[
            pl.ds(pair * rows + row, ch, stride=stride), :
        ]
    peers = 2
    for there in (has_z, has_low, has_high):
        peers = peers + there.astype(jnp.int32)
    pl.semaphore_wait(barrier, peers)

    psi_copy().start()
    send_block(0, pair)

    def put_weight(b, k, matrix):
        at = pl.ds(k % quad * ch, ch)
        place = k // quad
        high, low = halves(matrix)
        w_stack[b, at, pl.ds(place * ch, ch)] = high
        w_stack[b, at, pl.ds((2 + place) * ch, ch)] = low
        w_stack[b, at, pl.ds((4 + place) * ch, ch)] = high

    at_row = lax.broadcasted_iota(jnp.int32, (ch, ch), 0)
    at_col = lax.broadcasted_iota(jnp.int32, (ch, ch), 1)
    momenta = angular[...].astype(F32)
    momenta = 0.5 * momenta * (momenta + 1.0)
    weights[pair, pl.ds(side, 2)] = momenta
    loads[1].wait()
    loads[2].wait()
    for k in range(quad):
        both = []
        for index in (k, k + quad):
            matrix = (0.5 * selection[0, index].astype(F32)) * (coupling[index] + coupling[index].T)
            weights[pair, pl.ds(side + 2 + index, 1)] = jnp.sum(
                jnp.where(at_row == at_col, matrix, 0.0), axis=0, keepdims=True
            )
            both.append(matrix)
        weights[pair, pl.ds(k * ch, ch)] = jnp.where(at_row < at_col, both[0], both[1])
        put_weight(pair, k, both[0])
        put_weight(pair, k + quad, both[1])
    for a in range(2):
        weights[pair, pl.ds((quad + a) * ch, ch)] = dipole[a]
    weight_copy().start()

    def unpack(b):
        for k in range(quad):
            packed = weights[b, pl.ds(k * ch, ch)]
            for index, keep in ((k, at_row < at_col), (k + quad, at_row > at_col)):
                kept = jnp.where(keep, packed, 0.0)
                diagonal = weights[b, pl.ds(side + 2 + index, 1)]
                put_weight(b, index, jnp.where(at_row == at_col, diagonal, kept + kept.T))

    def spread(b):
        for a in range(2):
            vector = weights[b, pl.ds(side + a, 1)]
            central[b, a] = jnp.broadcast_to(vector, (cols, ch)).T

    for step in range(TAYLOR):
        for b in range(2):
            @pl.when(jnp.logical_not(has_low))
            def _(step=step, b=b):
                state[step, b, :, pl.ds(0, edge)] = jnp.zeros((ch, edge), F32)

            @pl.when(jnp.logical_not(has_high))
            def _(step=step, b=b):
                state[step, b, :, pl.ds(edge + width, edge)] = jnp.zeros((ch, edge), F32)

        @pl.when(jnp.logical_not(has_z))
        def _(step=step):
            near[step, 2 * core] = jnp.zeros((ch, width), F32)

    @pl.when(jnp.logical_and(core == 0, jnp.logical_not(has_z)))
    def _():
        lower[0] = jnp.zeros((2 * ch, ch), F32)

    def stack_dipoles(b):
        for a in range(2):
            at = pl.ds(a * ch, ch)
            for part_at, matrix in ((0, weights[b, pl.ds((quad + a) * ch, ch)]), (1, lower[b, pl.ds(a * ch, ch)].T)):
                high, low = halves(matrix)
                d_stack[b, at, pl.ds(part_at * ch, ch)] = high
                d_stack[b, at, pl.ds((2 + part_at) * ch, ch)] = low
                d_stack[b, at, pl.ds((4 + part_at) * ch, ch)] = high

    span = ROWS * cols

    def radii(at):
        index = lax.broadcasted_iota(jnp.int32, (1, span), 1)
        row = tile * rows + at * ROWS + index // cols
        one = radius_start + grid_step * row.astype(F32)
        two = radius_start + grid_step * (index % cols).astype(F32)
        return one, two

    def multipoles(step, b):
        def body(at, carry):
            one, two = radii(at)
            inverse = 1.0 / jnp.maximum(one, two)
            ratio = jnp.minimum(one, two) * inverse
            power = ratio
            for _ in range(quad - 1):
                power = power * ratio
            value = state[step, b, :, pl.ds(pl.multiple_of(edge + at * span, cols), span)]
            stacked = three_pass([value, power * value])
            product = jnp.dot(w_stack[b], stacked, preferred_element_type=F32)
            result = product[(quad - 1) * ch:]
            for a in range(quad - 2, -1, -1):
                result = product[a * ch:(a + 1) * ch] + ratio * result
            part[b, :, pl.ds(pl.multiple_of(at * span, cols), span)] = result * inverse
            return carry

        lax.fori_loop(0, rows // ROWS, body, 0)

    def finish(step, b, scale):
        strength = field[0]
        lane_at = lax.broadcasted_iota(jnp.int32, (1, cols), 1)

        def body(at, carry):
            one, two = radii(at)
            here = pl.ds(pl.multiple_of(at * span, cols), span)
            up = near[step, b + 1, :, here]
            down = near[step, b, :, here]
            product = jnp.dot(d_stack[b], three_pass([up, down]), preferred_element_type=F32)
            dipole_term = (strength * one) * product[:ch] + (strength * two) * product[ch:]

            def window(offset):
                start = pl.multiple_of(at * span + (HALO + offset) * cols, cols)
                return state[step, b, :, pl.ds(start, span)]

            value = window(0)
            around = 16.0 * (window(-1) + window(1)) - (window(-2) + window(2))
            pieces = []
            for r in range(ROWS):
                line = value[:, r * cols:(r + 1) * cols]

                def moved(by):
                    rolled = pltpu.roll(line, by % cols, 1)
                    inside = lane_at >= by if by > 0 else lane_at < cols + by
                    return jnp.where(inside, rolled, 0.0)

                pieces.append(16.0 * (moved(1) + moved(-1)) - (moved(2) + moved(-2)))
            around = around + jnp.concatenate(pieces, axis=1)
            factor = -0.5 / (12.0 * grid_step * grid_step)
            inv_one, inv_two = 1.0 / one, 1.0 / two
            c_one = jnp.concatenate([central[b, 0]] * ROWS, axis=1)
            c_two = jnp.concatenate([central[b, 1]] * ROWS, axis=1)
            centre = (
                (-60.0 * factor - 2.0 * inv_one - 2.0 * inv_two)
                + c_one * (inv_one * inv_one)
                + c_two * (inv_two * inv_two)
            )
            applied = factor * around + centre * value + part[b, :, here] + dipole_term
            term = scale * applied
            start = pl.multiple_of(edge + at * span, cols)
            state[step + 1, b, :, pl.ds(start, span)] = term
            which = (step + 1) % 2
            totals[which, b, :, here] = totals[which, b, :, here] + term
            return carry

        lax.fori_loop(0, rows // ROWS, body, 0)

    spread(pair)
    multipoles(0, pair)
    psi_copy().wait_recv()
    send_block(0, other)
    for b in range(2):
        totals[0, b] = state[0, b, :, mid]
        totals[1, b] = jnp.zeros((ch, width), F32)
    weight_copy().wait_recv()

    @pl.when(core == 0)
    def _():
        dcore_low(0).start()
        dcore_low(1).start()

    @pl.when(core == 1)
    def _():
        dcore_high().start()

        @pl.when(has_z)
        def _():
            dz_copy().start()

    unpack(other)
    spread(other)
    multipoles(0, other)

    @pl.when(core == 1)
    def _():
        dcore_low(0).wait_recv()
        dcore_low(1).wait_recv()

    @pl.when(core == 0)
    def _():
        dcore_high().wait_recv()

        @pl.when(has_z)
        def _():
            dz_copy().wait_recv()

    stack_dipoles(0)
    stack_dipoles(1)

    def order(step, carry):
        @pl.when(step > 0)
        def _():
            multipoles(step, other)

        @pl.when(jnp.logical_and(step > 0, step < TAYLOR - 1))
        def _():
            multipoles(step, pair)

        sign = ((2 * ((step + 1) % 2) - 1) * (2 * pair - 1)).astype(F32)
        scale = sign * (time_step / (step + 1).astype(F32))
        core_copy(step, 0).wait_recv()
        core_copy(step, 1).wait_recv()

        @pl.when(has_z)
        def _():
            z_copy(step).wait_recv()

        for b in (other, pair):
            wait_halo(step, b)
            finish(step, b, scale)

            @pl.when(step < TAYLOR - 1)
            def _():
                send_block(step + 1, b)

            if b is other:
                @pl.when(step >= TAYLOR - 2)
                def _():
                    back_copy((step + 1) % 2).start()

                @pl.when(step == TAYLOR - 1)
                def _():
                    multipoles(step, pair)
        return carry

    lax.fori_loop(0, TAYLOR, order, 0)

    for which, component in ((0, pair), (1, other)):
        back_copy(1 - which).wait_recv()
        for row in range(rows):
            here = pl.ds(row * cols, cols)
            out[pl.ds(component * rows + row, ch, stride=stride), :] = (
                totals[which, pair, :, here] + from_pair[1 - which, :, here]
            )

    psi_copy().wait_send()
    weight_copy().wait_send()
    for step in range(TAYLOR):
        for b in range(2):
            wait_sent(step, b)

    @pl.when(core == 0)
    def _():
        dcore_low(0).wait_send()
        dcore_low(1).wait_send()

    @pl.when(core == 1)
    def _():
        dcore_high().wait_send()

        @pl.when(has_z)
        def _():
            dz_copy().wait_send()

    back_copy(0).wait_send()
    back_copy(1).wait_send()


def per_device(blocks, tiles, wavefunction, l_table, coupling, selection, dipole, field):
    ch, parts, rows, cols = wavefunction.shape
    width = rows * cols
    nmp = coupling.shape[1]
    edge = HALO * cols
    wave = wavefunction.reshape(ch * parts * rows, cols)
    message = (nmp // 2 + 2) * ch + -(-(nmp + 2) // 8) * 8
    there = pl.BlockSpec(memory_space=pl.ANY)
    vmem = pl.BlockSpec(memory_space=pltpu.VMEM)
    smem = pl.BlockSpec(memory_space=pltpu.SMEM)
    dma = pltpu.SemaphoreType.DMA
    result = pl.pallas_call(
        functools.partial(kernel, blocks, tiles, rows),
        out_shape=jax.ShapeDtypeStruct(wave.shape, F32),
        in_specs=[there, vmem, there, there, smem, smem],
        out_specs=vmem,
        scratch_shapes=[
            pltpu.VMEM(wave.shape, F32),
            pltpu.VMEM((nmp, ch, ch), F32),
            pltpu.VMEM((2, ch, ch), F32),
            pltpu.VMEM((ch, width), F32),
            pltpu.VMEM((TAYLOR + 1, 2, ch, width + 2 * edge), F32),
            pltpu.VMEM((TAYLOR, 3, ch, width), F32),
            pltpu.VMEM((2, message, ch), F32),
            pltpu.VMEM((2, 2, ch, cols), F32),
            pltpu.VMEM((2, 2 * ch, ch), F32),
            pltpu.VMEM((2, nmp // 2 * ch, 6 * ch), BF16),
            pltpu.VMEM((2, 2 * ch, 6 * ch), BF16),
            pltpu.VMEM((2, ch, width), F32),
            pltpu.VMEM((2, 2, ch, width), F32),
            pltpu.VMEM((2, ch, width), F32),
            dma((3,)),
            dma((2,)),
            dma((2,)),
            dma((TAYLOR, 2, 2)),
            dma((TAYLOR, 2)),
            dma((TAYLOR, 2, 2)),
            dma((TAYLOR, 2, 2)),
            dma((2, 2)),
            dma((2,)),
            dma((2, 2)),
        ],
        compiler_params=pltpu.CompilerParams(
            collective_id=0, has_side_effects=True, vmem_limit_bytes=48 * 1024 * 1024
        ),
    )(wave, l_table.T, coupling[0], dipole[0], selection, field)
    return result.reshape(wavefunction.shape)


def solution(mesh):
    placed = (
        P("lblk", None, "tile", None),
        P("lblk", None),
        P("lblk", None, None, None),
        P("lblk", None),
        P("lblk", None, None, None),
        P(),
    )
    return jax.shard_map(
        functools.partial(per_device, mesh.shape["lblk"], mesh.shape["tile"]),
        mesh=mesh,
        in_specs=placed,
        out_specs=P("lblk", None, "tile", None),
        check_vma=False,
    )
```

```python
import functools

import jax
import jax.numpy as jnp
from jax import lax
from jax.experimental import pallas as pl
from jax.experimental.pallas import tpu as pltpu
from jax.sharding import PartitionSpec as P

TAYLOR = 4
time_step = 0.03
grid_step = 0.5
radius_start = 8.0
F32 = jnp.float32
BF16 = jnp.bfloat16
MESH = pl.DeviceIdType.MESH
HALO = 2
ROWS = 2


def halves(value):
    high = value.astype(BF16)
    return high, (value - high.astype(F32)).astype(BF16)


def three_pass(value_list):
    pairs = [halves(value) for value in value_list]
    high = [pair[0] for pair in pairs]
    return jnp.concatenate(high + high + [pair[1] for pair in pairs], axis=0)


def kernel(
    blocks, tiles, rows, wave_in, angular_in, coupling_in, dipole_in, selection, field, out,
    wave, angular, coupling, dipole, start_other,
    state, near, weights, central, lower, w_stack, d_stack, part, totals, from_pair,
    load_sem, psi_sem, wgt_sem, relay_sem, core_sem, z_sem, down_sem, up_sem, dcore_sem, dz_sem, back_sem,
):
    ch = coupling.shape[1]
    nmp = coupling.shape[0]
    quad = nmp // 2
    cols = wave.shape[1]
    width = rows * cols
    stride = 2 * rows
    side = (quad + 2) * ch
    edge = HALO * cols
    mid = pl.ds(edge, width)
    span = ROWS * cols
    chunks = rows // ROWS

    me = lax.axis_index("lblk")
    tile = lax.axis_index("tile")
    core = me % 2
    pair = (me // 2) % 2
    other = 1 - pair
    quad_at = me // 4
    last_quad = blocks // 4 - 1
    to_pair = {"lblk": me + 2 - 4 * pair}
    to_core = {"lblk": me + 1 - 2 * core}
    to_z = {"lblk": me + 6 * core - 3}
    to_relay = {"tile": tile + 1 - 2 * (tile % 2)}
    to_low = {"tile": tile - 1}
    to_high = {"tile": tile + 1}
    has_z = jnp.logical_or(
        jnp.logical_and(core == 1, quad_at < last_quad), jnp.logical_and(core == 0, quad_at > 0)
    )
    has_low = tile > 0
    has_high = tile < tiles - 1

    def remote(src, dst, sems, target):
        return pltpu.make_async_remote_copy(
            src_ref=src, dst_ref=dst, send_sem=sems.at[0], recv_sem=sems.at[1],
            device_id=target, device_id_type=MESH,
        )

    def chunk_at(at, offset=0):
        return pl.ds(pl.multiple_of(offset + at * span, cols), span)

    def psi_copy(at):
        return remote(
            start_other.at[:, chunk_at(at)], state.at[0, pair, :, chunk_at(at, edge)],
            psi_sem.at[at], to_pair,
        )

    relayed = tiles % 2 == 0
    length = weights.shape[1] // 2 if relayed else weights.shape[1]
    half = pl.ds(pl.multiple_of(tile % 2 * length, 8), length) if relayed else pl.ds(0, length)

    def weight_copy():
        return remote(weights.at[pair, half], weights.at[pair, half], wgt_sem, to_pair)

    def relay_copy():
        return remote(weights.at[other, half], weights.at[other, half], relay_sem, to_relay)

    def core_copy(step, b):
        return remote(state.at[step, b, :, mid], near.at[step, core + b], core_sem.at[step, b], to_core)

    def z_copy(step, at):
        return remote(
            state.at[step, core, :, chunk_at(at, edge)],
            near.at[step, 2 * (1 - core), :, chunk_at(at)], z_sem.at[step, at], to_z,
        )

    def low_copy(step, b):
        return remote(
            state.at[step, b, :, pl.ds(edge, edge)], state.at[step, b, :, pl.ds(edge + width, edge)],
            down_sem.at[step, b], to_low,
        )

    def high_copy(step, b):
        return remote(
            state.at[step, b, :, pl.ds(width, edge)], state.at[step, b, :, pl.ds(0, edge)],
            up_sem.at[step, b], to_high,
        )

    def send_chunk(step, b, at):
        @pl.when(jnp.logical_and(b == core, has_z))
        def _():
            z_copy(step, at).start()

        @pl.when(jnp.logical_and(at == 0, has_low))
        def _():
            low_copy(step, b).start()

        @pl.when(jnp.logical_and(at == chunks - 1, has_high))
        def _():
            high_copy(step, b).start()

    def wait_sent(step, b):
        @pl.when(jnp.logical_and(b == core, has_z))
        def _():
            for at in range(chunks):
                z_copy(step, at).wait_send()

        @pl.when(has_low)
        def _():
            low_copy(step, b).wait_send()

        @pl.when(has_high)
        def _():
            high_copy(step, b).wait_send()

        core_copy(step, b).wait_send()

    def wait_halo(step, b):
        @pl.when(has_high)
        def _():
            low_copy(step, b).wait_recv()

        @pl.when(has_low)
        def _():
            high_copy(step, b).wait_recv()

    def back_copy(which, at):
        return remote(
            totals.at[which, other, :, chunk_at(at)], from_pair.at[which, :, chunk_at(at)],
            back_sem.at[which, at], to_pair,
        )

    def dcore_low(b):
        return remote(weights.at[b, pl.ds(quad * ch, 2 * ch)], lower.at[b], dcore_sem.at[b], to_core)

    def dcore_high():
        return remote(weights.at[0, pl.ds(quad * ch, 2 * ch)], lower.at[1], dcore_sem.at[1], to_core)

    def dz_copy():
        return remote(weights.at[1, pl.ds(quad * ch, 2 * ch)], lower.at[0], dz_sem, to_z)

    loads = [
        pltpu.make_async_copy(src, dst, load_sem.at[at])
        for at, (src, dst) in enumerate(((wave_in, wave), (coupling_in, coupling), (dipole_in, dipole), (angular_in, angular)))
    ]
    for load in loads:
        load.start()

    barrier = pltpu.get_barrier_semaphore()
    for target, there in (
        (to_pair, None), (to_core, None), (to_z, has_z), (to_low, has_low), (to_high, has_high),
    ):
        if there is None:
            pl.semaphore_signal(barrier, inc=1, device_id=target, device_id_type=MESH)
        else:
            @pl.when(there)
            def _(target=target):
                pl.semaphore_signal(barrier, inc=1, device_id=target, device_id_type=MESH)
    loads[0].wait()
    for row in range(rows):
        here = pl.ds(row * cols, cols)
        start_other[:, here] = wave[pl.ds(other * rows + row, ch, stride=stride), :]
        state[0, pair, :, pl.ds(edge + row * cols, cols)] = wave[
            pl.ds(pair * rows + row, ch, stride=stride), :
        ]
    peers = 2
    for there in (has_z, has_low, has_high):
        peers = peers + there.astype(jnp.int32)
    pl.semaphore_wait(barrier, peers)

    psi_copy(0).start()
    for at in range(chunks):
        send_chunk(0, pair, at)
    core_copy(0, pair).start()

    def put_weight(b, k, matrix):
        at = pl.ds(k % quad * ch, ch)
        place = k // quad
        high, low = halves(matrix)
        w_stack[b, at, pl.ds(place * ch, ch)] = high
        w_stack[b, at, pl.ds((2 + place) * ch, ch)] = low
        w_stack[b, at, pl.ds((4 + place) * ch, ch)] = high

    at_row = lax.broadcasted_iota(jnp.int32, (ch, ch), 0)
    at_col = lax.broadcasted_iota(jnp.int32, (ch, ch), 1)
    loads[3].wait()
    momenta = angular[...].astype(F32)
    momenta = 0.5 * momenta * (momenta + 1.0)
    weights[pair, pl.ds(side, 2)] = momenta
    loads[1].wait()
    loads[2].wait()
    for k in range(quad):
        both = []
        for index in (k, k + quad):
            matrix = (0.5 * selection[0, index].astype(F32)) * (coupling[index] + coupling[index].T)
            weights[pair, pl.ds(side + 2 + index, 1)] = jnp.sum(
                jnp.where(at_row == at_col, matrix, 0.0), axis=0, keepdims=True
            )
            both.append(matrix)
        weights[pair, pl.ds(k * ch, ch)] = jnp.where(at_row < at_col, both[0], both[1])
        put_weight(pair, k, both[0])
        put_weight(pair, k + quad, both[1])
    for a in range(2):
        weights[pair, pl.ds((quad + a) * ch, ch)] = dipole[a]
    weight_copy().start()
    for at in range(1, chunks):
        psi_copy(at).start()

    def unpack(b):
        for k in range(quad):
            packed = weights[b, pl.ds(k * ch, ch)]
            for index, keep in ((k, at_row < at_col), (k + quad, at_row > at_col)):
                kept = jnp.where(keep, packed, 0.0)
                diagonal = weights[b, pl.ds(side + 2 + index, 1)]
                put_weight(b, index, jnp.where(at_row == at_col, diagonal, kept + kept.T))

    def spread(b):
        for a in range(2):
            vector = weights[b, pl.ds(side + a, 1)]
            central[b, a] = jnp.broadcast_to(vector, (cols, ch)).T

    for step in range(TAYLOR):
        for b in range(2):
            @pl.when(jnp.logical_not(has_low))
            def _(step=step, b=b):
                state[step, b, :, pl.ds(0, edge)] = jnp.zeros((ch, edge), F32)

            @pl.when(jnp.logical_not(has_high))
            def _(step=step, b=b):
                state[step, b, :, pl.ds(edge + width, edge)] = jnp.zeros((ch, edge), F32)

        @pl.when(jnp.logical_not(has_z))
        def _(step=step):
            near[step, 2 * core] = jnp.zeros((ch, width), F32)

    @pl.when(jnp.logical_and(core == 0, jnp.logical_not(has_z)))
    def _():
        lower[0] = jnp.zeros((2 * ch, ch), F32)

    def stack_dipoles(b):
        for a in range(2):
            at = pl.ds(a * ch, ch)
            for part_at, matrix in ((0, weights[b, pl.ds((quad + a) * ch, ch)]), (1, lower[b, pl.ds(a * ch, ch)].T)):
                high, low = halves(matrix)
                d_stack[b, at, pl.ds(part_at * ch, ch)] = high
                d_stack[b, at, pl.ds((2 + part_at) * ch, ch)] = low
                d_stack[b, at, pl.ds((4 + part_at) * ch, ch)] = high

    def radii(at):
        index = lax.broadcasted_iota(jnp.int32, (1, span), 1)
        row = tile * rows + at * ROWS + index // cols
        one = radius_start + grid_step * row.astype(F32)
        two = radius_start + grid_step * (index % cols).astype(F32)
        return one, two

    def multipoles(step, b):
        def body(at, carry):
            one, two = radii(at)
            inverse = 1.0 / jnp.maximum(one, two)
            ratio = jnp.minimum(one, two) * inverse
            power = ratio
            for _ in range(quad - 1):
                power = power * ratio
            value = state[step, b, :, pl.ds(pl.multiple_of(edge + at * span, cols), span)]
            stacked = three_pass([value, power * value])
            product = jnp.dot(w_stack[b], stacked, preferred_element_type=F32)
            result = product[(quad - 1) * ch:]
            for a in range(quad - 2, -1, -1):
                result = product[a * ch:(a + 1) * ch] + ratio * result
            part[b, :, pl.ds(pl.multiple_of(at * span, cols), span)] = result * inverse
            return carry

        lax.fori_loop(0, rows // ROWS, body, 0)

    def finish(step, b, scale):
        strength = field[0]
        lane_at = lax.broadcasted_iota(jnp.int32, (1, cols), 1)

        def body(at, carry):
            @pl.when(jnp.logical_and(b == core, has_z))
            def _():
                z_copy(step, at).wait_recv()

            one, two = radii(at)
            here = pl.ds(pl.multiple_of(at * span, cols), span)
            up = near[step, b + 1, :, here]
            down = near[step, b, :, here]
            product = jnp.dot(d_stack[b], three_pass([up, down]), preferred_element_type=F32)
            dipole_term = (strength * one) * product[:ch] + (strength * two) * product[ch:]

            def window(offset):
                start = pl.multiple_of(at * span + (HALO + offset) * cols, cols)
                return state[step, b, :, pl.ds(start, span)]

            value = window(0)
            around = 16.0 * (window(-1) + window(1)) - (window(-2) + window(2))
            pieces = []
            for r in range(ROWS):
                line = value[:, r * cols:(r + 1) * cols]

                def moved(by):
                    rolled = pltpu.roll(line, by % cols, 1)
                    inside = lane_at >= by if by > 0 else lane_at < cols + by
                    return jnp.where(inside, rolled, 0.0)

                pieces.append(16.0 * (moved(1) + moved(-1)) - (moved(2) + moved(-2)))
            around = around + jnp.concatenate(pieces, axis=1)
            factor = -0.5 / (12.0 * grid_step * grid_step)
            inv_one, inv_two = 1.0 / one, 1.0 / two
            c_one = jnp.concatenate([central[b, 0]] * ROWS, axis=1)
            c_two = jnp.concatenate([central[b, 1]] * ROWS, axis=1)
            centre = (
                (-60.0 * factor - 2.0 * inv_one - 2.0 * inv_two)
                + c_one * (inv_one * inv_one)
                + c_two * (inv_two * inv_two)
            )
            applied = factor * around + centre * value + part[b, :, here] + dipole_term
            term = scale * applied
            start = pl.multiple_of(edge + at * span, cols)
            state[step + 1, b, :, pl.ds(start, span)] = term
            which = (step + 1) % 2
            totals[which, b, :, here] = totals[which, b, :, here] + term

            @pl.when(step < TAYLOR - 1)
            def _():
                send_chunk(step + 1, b, at)

            @pl.when(jnp.logical_and(step >= TAYLOR - 2, b == other))
            def _():
                back_copy(which, at).start()
            return carry

        lax.fori_loop(0, rows // ROWS, body, 0)

    spread(pair)
    multipoles(0, pair)
    weight_copy().wait_recv()
    if relayed:
        relay_copy().start()

    def pass_on(at):
        psi_copy(at).wait_recv()
        send_chunk(0, other, at)

    for at in range(chunks // 2):
        pass_on(at)
    if relayed:
        relay_copy().wait_recv()

    @pl.when(core == 0)
    def _():
        dcore_low(0).start()
        dcore_low(1).start()

    @pl.when(core == 1)
    def _():
        dcore_high().start()

        @pl.when(has_z)
        def _():
            dz_copy().start()

    unpack(other)
    spread(other)
    for at in range(chunks // 2, chunks):
        pass_on(at)
    core_copy(0, other).start()
    for b in range(2):
        totals[0, b] = state[0, b, :, mid]
        totals[1, b] = jnp.zeros((ch, width), F32)
    multipoles(0, other)

    @pl.when(core == 1)
    def _():
        dcore_low(0).wait_recv()
        dcore_low(1).wait_recv()

    @pl.when(core == 0)
    def _():
        dcore_high().wait_recv()

        @pl.when(has_z)
        def _():
            dz_copy().wait_recv()

    stack_dipoles(0)
    stack_dipoles(1)

    def order(step, carry):
        last = step == TAYLOR - 1
        first = jnp.where(last, other, core)
        second = 1 - first

        @pl.when(step > 0)
        def _():
            multipoles(step, first)

        @pl.when(jnp.logical_and(step > 0, step < TAYLOR - 1))
        def _():
            multipoles(step, second)

        sign = ((2 * ((step + 1) % 2) - 1) * (2 * pair - 1)).astype(F32)
        scale = sign * (time_step / (step + 1).astype(F32))
        core_copy(step, 0).wait_recv()
        core_copy(step, 1).wait_recv()
        for b in (first, second):
            wait_halo(step, b)
            finish(step, b, scale)

            @pl.when(step < TAYLOR - 1)
            def _():
                core_copy(step + 1, b).start()

            if b is first:
                @pl.when(last)
                def _():
                    multipoles(step, second)
        return carry

    lax.fori_loop(0, TAYLOR, order, 0)

    for which, component in ((0, pair), (1, other)):
        for at in range(chunks):
            back_copy(1 - which, at).wait_recv()
            for row in range(at * ROWS, (at + 1) * ROWS):
                here = pl.ds(row * cols, cols)
                out[pl.ds(component * rows + row, ch, stride=stride), :] = (
                    totals[which, pair, :, here] + from_pair[1 - which, :, here]
                )

    for at in range(chunks):
        psi_copy(at).wait_send()
        back_copy(0, at).wait_send()
        back_copy(1, at).wait_send()
    if relayed:
        relay_copy().wait_send()
    weight_copy().wait_send()
    for step in range(TAYLOR):
        for b in range(2):
            wait_sent(step, b)

    @pl.when(core == 0)
    def _():
        dcore_low(0).wait_send()
        dcore_low(1).wait_send()

    @pl.when(core == 1)
    def _():
        dcore_high().wait_send()

        @pl.when(has_z)
        def _():
            dz_copy().wait_send()


def per_device(blocks, tiles, wavefunction, l_table, coupling, selection, dipole, field):
    ch, parts, rows, cols = wavefunction.shape
    width = rows * cols
    nmp = coupling.shape[1]
    edge = HALO * cols
    wave = wavefunction.reshape(ch * parts * rows, cols)
    message = (nmp // 2 + 2) * ch + -(-(nmp + 2) // 8) * 8
    there = pl.BlockSpec(memory_space=pltpu.HBM)
    chunks = rows // ROWS
    vmem = pl.BlockSpec(memory_space=pltpu.VMEM)
    smem = pl.BlockSpec(memory_space=pltpu.SMEM)
    dma = pltpu.SemaphoreType.DMA
    result = pl.pallas_call(
        functools.partial(kernel, blocks, tiles, rows),
        out_shape=jax.ShapeDtypeStruct(wave.shape, F32),
        in_specs=[there, there, there, there, smem, smem],
        out_specs=vmem,
        scratch_shapes=[
            pltpu.VMEM(wave.shape, F32),
            pltpu.VMEM((2, ch), jnp.int32),
            pltpu.VMEM((nmp, ch, ch), F32),
            pltpu.VMEM((2, ch, ch), F32),
            pltpu.VMEM((ch, width), F32),
            pltpu.VMEM((TAYLOR + 1, 2, ch, width + 2 * edge), F32),
            pltpu.VMEM((TAYLOR, 3, ch, width), F32),
            pltpu.VMEM((2, message, ch), F32),
            pltpu.VMEM((2, 2, ch, cols), F32),
            pltpu.VMEM((2, 2 * ch, ch), F32),
            pltpu.VMEM((2, nmp // 2 * ch, 6 * ch), BF16),
            pltpu.VMEM((2, 2 * ch, 6 * ch), BF16),
            pltpu.VMEM((2, ch, width), F32),
            pltpu.VMEM((2, 2, ch, width), F32),
            pltpu.VMEM((2, ch, width), F32),
            dma((4,)),
            dma((chunks, 2)),
            dma((2,)),
            dma((2,)),
            dma((TAYLOR, 2, 2)),
            dma((TAYLOR, chunks, 2)),
            dma((TAYLOR, 2, 2)),
            dma((TAYLOR, 2, 2)),
            dma((2, 2)),
            dma((2,)),
            dma((2, chunks, 2)),
        ],
        compiler_params=pltpu.CompilerParams(
            collective_id=0, has_side_effects=True, vmem_limit_bytes=63 * 1024 * 1024
        ),
    )(wave, l_table.T, coupling[0], dipole[0], selection, field)
    return result.reshape(wavefunction.shape)


def solution(mesh):
    placed = (
        P("lblk", None, "tile", None),
        P("lblk", None),
        P("lblk", None, None, None),
        P("lblk", None),
        P("lblk", None, None, None),
        P(),
    )
    return jax.shard_map(
        functools.partial(per_device, mesh.shape["lblk"], mesh.shape["tile"]),
        mesh=mesh,
        in_specs=placed,
        out_specs=P("lblk", None, "tile", None),
        check_vma=False,
    )
```

```python
import functools

import jax
import jax.numpy as jnp
from jax import lax
from jax.experimental import pallas as pl
from jax.experimental.pallas import tpu as pltpu
from jax.sharding import PartitionSpec as P

TAYLOR = 4
time_step = 0.03
grid_step = 0.5
radius_start = 8.0
F32 = jnp.float32
BF16 = jnp.bfloat16
MESH = pl.DeviceIdType.MESH
HALO = 2
ROWS = 2


def halves(value):
    high = value.astype(BF16)
    return high, (value - high.astype(F32)).astype(BF16)


def three_pass(value_list):
    pairs = [halves(value) for value in value_list]
    high = [pair[0] for pair in pairs]
    return jnp.concatenate(high + high + [pair[1] for pair in pairs], axis=0)


def kernel(
    blocks, tiles, rows, wave_in, angular_in, coupling_in, dipole_in, selection, field, mine_out, theirs_out,
    mine, theirs, wave, angular, coupling, dipole, start_other,
    state, near, weights, central, lower, w_stack, d_stack, part, totals, from_pair,
    load_sem, store_sem, psi_sem, wgt_sem, relay_sem, core_sem, z_sem, down_sem, up_sem, dcore_sem, dz_sem, back_sem,
):
    ch = coupling.shape[1]
    nmp = coupling.shape[0]
    quad = nmp // 2
    cols = wave.shape[1]
    width = rows * cols
    stride = 2 * rows
    side = (quad + 2) * ch
    edge = HALO * cols
    mid = pl.ds(edge, width)
    span = ROWS * cols
    chunks = rows // ROWS

    me = lax.axis_index("lblk")
    tile = lax.axis_index("tile")
    core = me % 2
    pair = (me // 2) % 2
    other = 1 - pair
    quad_at = me // 4
    last_quad = blocks // 4 - 1
    to_pair = {"lblk": me + 2 - 4 * pair}
    to_core = {"lblk": me + 1 - 2 * core}
    to_z = {"lblk": me + 6 * core - 3}
    to_relay = {"tile": tile + 1 - 2 * (tile % 2)}
    to_low = {"tile": tile - 1}
    to_high = {"tile": tile + 1}
    has_z = jnp.logical_or(
        jnp.logical_and(core == 1, quad_at < last_quad), jnp.logical_and(core == 0, quad_at > 0)
    )
    has_low = tile > 0
    has_high = tile < tiles - 1

    def remote(src, dst, sems, target):
        return pltpu.make_async_remote_copy(
            src_ref=src, dst_ref=dst, send_sem=sems.at[0], recv_sem=sems.at[1],
            device_id=target, device_id_type=MESH,
        )

    def chunk_at(at, offset=0):
        return pl.ds(pl.multiple_of(offset + at * span, cols), span)

    def psi_copy(at):
        return remote(
            start_other.at[:, chunk_at(at)], state.at[0, pair, :, chunk_at(at, edge)],
            psi_sem.at[at], to_pair,
        )

    relayed = tiles % 2 == 0
    length = weights.shape[1] // 2 if relayed else weights.shape[1]
    half = pl.ds(pl.multiple_of(tile % 2 * length, 8), length) if relayed else pl.ds(0, length)

    def weight_copy():
        return remote(weights.at[pair, half], weights.at[pair, half], wgt_sem, to_pair)

    def relay_copy():
        return remote(weights.at[other, half], weights.at[other, half], relay_sem, to_relay)

    def core_copy(step, b):
        return remote(state.at[step, b, :, mid], near.at[step, core + b], core_sem.at[step, b], to_core)

    def z_copy(step, at):
        return remote(
            state.at[step, core, :, chunk_at(at, edge)],
            near.at[step, 2 * (1 - core), :, chunk_at(at)], z_sem.at[step, at], to_z,
        )

    def low_copy(step, b):
        return remote(
            state.at[step, b, :, pl.ds(edge, edge)], state.at[step, b, :, pl.ds(edge + width, edge)],
            down_sem.at[step, b], to_low,
        )

    def high_copy(step, b):
        return remote(
            state.at[step, b, :, pl.ds(width, edge)], state.at[step, b, :, pl.ds(0, edge)],
            up_sem.at[step, b], to_high,
        )

    def send_chunk(step, b, at):
        @pl.when(jnp.logical_and(b == core, has_z))
        def _():
            z_copy(step, at).start()

        @pl.when(jnp.logical_and(at == 0, has_low))
        def _():
            low_copy(step, b).start()

        @pl.when(jnp.logical_and(at == chunks - 1, has_high))
        def _():
            high_copy(step, b).start()

    def wait_sent(step, b):
        @pl.when(jnp.logical_and(b == core, has_z))
        def _():
            for at in range(chunks):
                z_copy(step, at).wait_send()

        @pl.when(has_low)
        def _():
            low_copy(step, b).wait_send()

        @pl.when(has_high)
        def _():
            high_copy(step, b).wait_send()

        core_copy(step, b).wait_send()

    def wait_halo(step, b):
        @pl.when(has_high)
        def _():
            low_copy(step, b).wait_recv()

        @pl.when(has_low)
        def _():
            high_copy(step, b).wait_recv()

    def back_copy(which, at):
        return remote(
            totals.at[which, other, :, chunk_at(at)], from_pair.at[which, :, chunk_at(at)],
            back_sem.at[which, at], to_pair,
        )

    def dcore_low(b):
        return remote(weights.at[b, pl.ds(quad * ch, 2 * ch)], lower.at[b], dcore_sem.at[b], to_core)

    def dcore_high():
        return remote(weights.at[0, pl.ds(quad * ch, 2 * ch)], lower.at[1], dcore_sem.at[1], to_core)

    def dz_copy():
        return remote(weights.at[1, pl.ds(quad * ch, 2 * ch)], lower.at[0], dz_sem, to_z)

    loads = [
        pltpu.make_async_copy(src, dst, load_sem.at[at])
        for at, (src, dst) in enumerate(((wave_in, wave), (coupling_in, coupling), (dipole_in, dipole), (angular_in, angular)))
    ]
    for load in loads:
        load.start()

    barrier = pltpu.get_barrier_semaphore()
    for target, there in (
        (to_pair, None), (to_core, None), (to_z, has_z), (to_low, has_low), (to_high, has_high),
    ):
        if there is None:
            pl.semaphore_signal(barrier, inc=1, device_id=target, device_id_type=MESH)
        else:
            @pl.when(there)
            def _(target=target):
                pl.semaphore_signal(barrier, inc=1, device_id=target, device_id_type=MESH)
    loads[0].wait()
    for row in range(rows):
        here = pl.ds(row * cols, cols)
        start_other[:, here] = wave[pl.ds(other * rows + row, ch, stride=stride), :]
        state[0, pair, :, pl.ds(edge + row * cols, cols)] = wave[
            pl.ds(pair * rows + row, ch, stride=stride), :
        ]
    peers = 2
    for there in (has_z, has_low, has_high):
        peers = peers + there.astype(jnp.int32)
    pl.semaphore_wait(barrier, peers)

    psi_copy(0).start()
    for at in range(chunks):
        send_chunk(0, pair, at)
    core_copy(0, pair).start()

    def put_weight(b, k, matrix):
        at = pl.ds(k % quad * ch, ch)
        place = k // quad
        high, low = halves(matrix)
        w_stack[b, at, pl.ds(place * ch, ch)] = high
        w_stack[b, at, pl.ds((2 + place) * ch, ch)] = low
        w_stack[b, at, pl.ds((4 + place) * ch, ch)] = high

    at_row = lax.broadcasted_iota(jnp.int32, (ch, ch), 0)
    at_col = lax.broadcasted_iota(jnp.int32, (ch, ch), 1)
    loads[3].wait()
    momenta = angular[...].astype(F32)
    momenta = 0.5 * momenta * (momenta + 1.0)
    weights[pair, pl.ds(side, 2)] = momenta
    loads[1].wait()
    loads[2].wait()
    for k in range(quad):
        both = []
        for index in (k, k + quad):
            matrix = (0.5 * selection[0, index].astype(F32)) * (coupling[index] + coupling[index].T)
            weights[pair, pl.ds(side + 2 + index, 1)] = jnp.sum(
                jnp.where(at_row == at_col, matrix, 0.0), axis=0, keepdims=True
            )
            both.append(matrix)
        weights[pair, pl.ds(k * ch, ch)] = jnp.where(at_row < at_col, both[0], both[1])
        put_weight(pair, k, both[0])
        put_weight(pair, k + quad, both[1])
    for a in range(2):
        weights[pair, pl.ds((quad + a) * ch, ch)] = dipole[a]
    weight_copy().start()
    for at in range(1, chunks):
        psi_copy(at).start()

    def unpack(b):
        for k in range(quad):
            packed = weights[b, pl.ds(k * ch, ch)]
            for index, keep in ((k, at_row < at_col), (k + quad, at_row > at_col)):
                kept = jnp.where(keep, packed, 0.0)
                diagonal = weights[b, pl.ds(side + 2 + index, 1)]
                put_weight(b, index, jnp.where(at_row == at_col, diagonal, kept + kept.T))

    def spread(b):
        for a in range(2):
            vector = weights[b, pl.ds(side + a, 1)]
            central[b, a] = jnp.broadcast_to(vector, (cols, ch)).T

    for step in range(TAYLOR):
        for b in range(2):
            @pl.when(jnp.logical_not(has_low))
            def _(step=step, b=b):
                state[step, b, :, pl.ds(0, edge)] = jnp.zeros((ch, edge), F32)

            @pl.when(jnp.logical_not(has_high))
            def _(step=step, b=b):
                state[step, b, :, pl.ds(edge + width, edge)] = jnp.zeros((ch, edge), F32)

        @pl.when(jnp.logical_not(has_z))
        def _(step=step):
            near[step, 2 * core] = jnp.zeros((ch, width), F32)

    @pl.when(jnp.logical_and(core == 0, jnp.logical_not(has_z)))
    def _():
        lower[0] = jnp.zeros((2 * ch, ch), F32)

    def stack_dipoles(b):
        for a in range(2):
            at = pl.ds(a * ch, ch)
            for part_at, matrix in ((0, weights[b, pl.ds((quad + a) * ch, ch)]), (1, lower[b, pl.ds(a * ch, ch)].T)):
                high, low = halves(matrix)
                d_stack[b, at, pl.ds(part_at * ch, ch)] = high
                d_stack[b, at, pl.ds((2 + part_at) * ch, ch)] = low
                d_stack[b, at, pl.ds((4 + part_at) * ch, ch)] = high

    def radii(at):
        index = lax.broadcasted_iota(jnp.int32, (1, span), 1)
        row = tile * rows + at * ROWS + index // cols
        one = radius_start + grid_step * row.astype(F32)
        two = radius_start + grid_step * (index % cols).astype(F32)
        return one, two

    def multipoles(step, b):
        def body(at, carry):
            one, two = radii(at)
            inverse = 1.0 / jnp.maximum(one, two)
            ratio = jnp.minimum(one, two) * inverse
            power = ratio
            for _ in range(quad - 1):
                power = power * ratio
            value = state[step, b, :, pl.ds(pl.multiple_of(edge + at * span, cols), span)]
            stacked = three_pass([value, power * value])
            product = jnp.dot(w_stack[b], stacked, preferred_element_type=F32)
            result = product[(quad - 1) * ch:]
            for a in range(quad - 2, -1, -1):
                result = product[a * ch:(a + 1) * ch] + ratio * result
            part[b, :, pl.ds(pl.multiple_of(at * span, cols), span)] = result * inverse
            return carry

        lax.fori_loop(0, rows // ROWS, body, 0, unroll=True)

    def finish(step, b, scale):
        strength = field[0]
        lane_at = lax.broadcasted_iota(jnp.int32, (1, cols), 1)

        def body(at, carry):
            @pl.when(jnp.logical_and(b == core, has_z))
            def _():
                z_copy(step, at).wait_recv()

            one, two = radii(at)
            here = pl.ds(pl.multiple_of(at * span, cols), span)
            up = near[step, b + 1, :, here]
            down = near[step, b, :, here]
            product = jnp.dot(d_stack[b], three_pass([up, down]), preferred_element_type=F32)
            dipole_term = (strength * one) * product[:ch] + (strength * two) * product[ch:]

            def window(offset):
                start = pl.multiple_of(at * span + (HALO + offset) * cols, cols)
                return state[step, b, :, pl.ds(start, span)]

            value = window(0)
            around = 16.0 * (window(-1) + window(1)) - (window(-2) + window(2))
            pieces = []
            for r in range(ROWS):
                line = value[:, r * cols:(r + 1) * cols]

                def moved(by):
                    rolled = pltpu.roll(line, by % cols, 1)
                    inside = lane_at >= by if by > 0 else lane_at < cols + by
                    return jnp.where(inside, rolled, 0.0)

                pieces.append(16.0 * (moved(1) + moved(-1)) - (moved(2) + moved(-2)))
            around = around + jnp.concatenate(pieces, axis=1)
            factor = -0.5 / (12.0 * grid_step * grid_step)
            inv_one, inv_two = 1.0 / one, 1.0 / two
            c_one = jnp.concatenate([central[b, 0]] * ROWS, axis=1)
            c_two = jnp.concatenate([central[b, 1]] * ROWS, axis=1)
            centre = (
                (-60.0 * factor - 2.0 * inv_one - 2.0 * inv_two)
                + c_one * (inv_one * inv_one)
                + c_two * (inv_two * inv_two)
            )
            applied = factor * around + centre * value + part[b, :, here] + dipole_term
            term = scale * applied
            start = pl.multiple_of(edge + at * span, cols)
            state[step + 1, b, :, pl.ds(start, span)] = term
            which = (step + 1) % 2
            totals[which, b, :, here] = totals[which, b, :, here] + term

            @pl.when(step < TAYLOR - 1)
            def _():
                send_chunk(step + 1, b, at)

            @pl.when(jnp.logical_and(step >= TAYLOR - 2, b == other))
            def _():
                back_copy(which, at).start()
            return carry

        lax.fori_loop(0, rows // ROWS, body, 0, unroll=True)

    spread(pair)
    multipoles(0, pair)
    weight_copy().wait_recv()
    if relayed:
        relay_copy().start()

    def pass_on(at):
        psi_copy(at).wait_recv()
        send_chunk(0, other, at)

    for at in range(chunks // 2):
        pass_on(at)
    if relayed:
        relay_copy().wait_recv()

    @pl.when(core == 0)
    def _():
        dcore_low(0).start()
        dcore_low(1).start()

    @pl.when(core == 1)
    def _():
        dcore_high().start()

        @pl.when(has_z)
        def _():
            dz_copy().start()

    unpack(other)
    spread(other)
    for at in range(chunks // 2, chunks):
        pass_on(at)
    core_copy(0, other).start()
    for b in range(2):
        totals[0, b] = state[0, b, :, mid]
        totals[1, b] = jnp.zeros((ch, width), F32)
    multipoles(0, other)

    @pl.when(core == 1)
    def _():
        dcore_low(0).wait_recv()
        dcore_low(1).wait_recv()

    @pl.when(core == 0)
    def _():
        dcore_high().wait_recv()

        @pl.when(has_z)
        def _():
            dz_copy().wait_recv()

    stack_dipoles(0)
    stack_dipoles(1)

    def order(step, carry):
        last = step == TAYLOR - 1
        first = jnp.where(last, other, core)
        second = 1 - first

        @pl.when(step > 0)
        def _():
            multipoles(step, first)

        @pl.when(jnp.logical_and(step > 0, step < TAYLOR - 1))
        def _():
            multipoles(step, second)

        sign = ((2 * ((step + 1) % 2) - 1) * (2 * pair - 1)).astype(F32)
        scale = sign * (time_step / (step + 1).astype(F32))
        core_copy(step, 0).wait_recv()
        core_copy(step, 1).wait_recv()
        for b in (first, second):
            wait_halo(step, b)
            finish(step, b, scale)

            @pl.when(step < TAYLOR - 1)
            def _():
                core_copy(step + 1, b).start()

            if b is first:
                @pl.when(last)
                def _():
                    multipoles(step, second)
        return carry

    lax.fori_loop(0, TAYLOR, order, 0)

    def rows_of(component, row):
        return pl.ds(component * rows + row, ch, stride=stride)

    for which, component in ((0, pair), (1, other)):
        for row in range(rows):
            mine[rows_of(component, row), :] = totals[which, pair, :, pl.ds(row * cols, cols)]
    stores = [
        pltpu.make_async_copy(src, dst, store_sem.at[at])
        for at, (src, dst) in enumerate(((mine, mine_out), (theirs, theirs_out)))
    ]
    stores[0].start()
    for which, component in ((1, pair), (0, other)):
        for at in range(chunks):
            back_copy(which, at).wait_recv()
            for row in range(at * ROWS, (at + 1) * ROWS):
                theirs[rows_of(component, row), :] = from_pair[which, :, pl.ds(row * cols, cols)]
    stores[1].start()
    for store in stores:
        store.wait()

    for at in range(chunks):
        psi_copy(at).wait_send()
        back_copy(0, at).wait_send()
        back_copy(1, at).wait_send()
    if relayed:
        relay_copy().wait_send()
    weight_copy().wait_send()
    for step in range(TAYLOR):
        for b in range(2):
            wait_sent(step, b)

    @pl.when(core == 0)
    def _():
        dcore_low(0).wait_send()
        dcore_low(1).wait_send()

    @pl.when(core == 1)
    def _():
        dcore_high().wait_send()

        @pl.when(has_z)
        def _():
            dz_copy().wait_send()


def per_device(blocks, tiles, wavefunction, l_table, coupling, selection, dipole, field):
    ch, parts, rows, cols = wavefunction.shape
    width = rows * cols
    nmp = coupling.shape[1]
    edge = HALO * cols
    wave = wavefunction.reshape(ch * parts * rows, cols)
    message = (nmp // 2 + 2) * ch + -(-(nmp + 2) // 8) * 8
    there = pl.BlockSpec(memory_space=pltpu.HBM)
    chunks = rows // ROWS
    smem = pl.BlockSpec(memory_space=pltpu.SMEM)
    dma = pltpu.SemaphoreType.DMA
    mine, theirs = pl.pallas_call(
        functools.partial(kernel, blocks, tiles, rows),
        out_shape=[jax.ShapeDtypeStruct(wave.shape, F32)] * 2,
        in_specs=[there, there, there, there, smem, smem],
        out_specs=[there, there],
        scratch_shapes=[
            pltpu.VMEM(wave.shape, F32),
            pltpu.VMEM(wave.shape, F32),
            pltpu.VMEM(wave.shape, F32),
            pltpu.VMEM((2, ch), jnp.int32),
            pltpu.VMEM((nmp, ch, ch), F32),
            pltpu.VMEM((2, ch, ch), F32),
            pltpu.VMEM((ch, width), F32),
            pltpu.VMEM((TAYLOR + 1, 2, ch, width + 2 * edge), F32),
            pltpu.VMEM((TAYLOR, 3, ch, width), F32),
            pltpu.VMEM((2, message, ch), F32),
            pltpu.VMEM((2, 2, ch, cols), F32),
            pltpu.VMEM((2, 2 * ch, ch), F32),
            pltpu.VMEM((2, nmp // 2 * ch, 6 * ch), BF16),
            pltpu.VMEM((2, 2 * ch, 6 * ch), BF16),
            pltpu.VMEM((2, ch, width), F32),
            pltpu.VMEM((2, 2, ch, width), F32),
            pltpu.VMEM((2, ch, width), F32),
            dma((4,)),
            dma((2,)),
            dma((chunks, 2)),
            dma((2,)),
            dma((2,)),
            dma((TAYLOR, 2, 2)),
            dma((TAYLOR, chunks, 2)),
            dma((TAYLOR, 2, 2)),
            dma((TAYLOR, 2, 2)),
            dma((2, 2)),
            dma((2,)),
            dma((2, chunks, 2)),
        ],
        compiler_params=pltpu.CompilerParams(
            collective_id=0, has_side_effects=True, vmem_limit_bytes=63 * 1024 * 1024
        ),
    )(wave, l_table.T, coupling[0], dipole[0], selection, field)
    return (mine + theirs).reshape(wavefunction.shape)


def solution(mesh):
    placed = (
        P("lblk", None, "tile", None),
        P("lblk", None),
        P("lblk", None, None, None),
        P("lblk", None),
        P("lblk", None, None, None),
        P(),
    )
    return jax.shard_map(
        functools.partial(per_device, mesh.shape["lblk"], mesh.shape["tile"]),
        mesh=mesh,
        in_specs=placed,
        out_specs=P("lblk", None, "tile", None),
        check_vma=False,
    )
```
